512 devices in a mesh: group: 16 (over z, core), member: 32 (over x, y).
Axes of the slice: x: 4, y: 8, z: 8, core: 2. Of those that a mesh axis runs over, the one named last changes fastest.
Arguments:
- entities: bfloat16 [524288, 256], P(('group', 'member')), may hold values from -1.5 to 1.5
- relations: bfloat16 [64, 256, 256], P('group'), may hold values from -0.375 to 0.375
- src_block: int32 [16, 32, 16], P('group'), may hold values from 0 to 7
- dst_member: int32 [16, 32, 16], P('group'), may hold values from 0 to 31, all different within a row
- dst_block: int32 [16, 32, 16], P('group'), may hold values from 0 to 7
- rel_id: int32 [16, 32, 16], P('group'), may hold values from 0 to 3
- neg_block: int32 [16, 32, 16], P(None, 'member'), may hold values from 0 to 7
- pos_mask: int32 [16, 32, 16, 128, 128], P('group', 'member'), may hold values 0 or 1
Outputs:
- entity_grad: float32 [524288, 256], P(('group', 'member'))
- relation_grad: float32 [64, 256, 256], P('group', 'member')
The draws below stay inside these ranges and needn't reach their ends.
Inputs may be any that keep to these rules, and one draw needn't show every extreme that they name: `dst_member`: the 16 tiles of one device name 16 different members.
All inputs are finite; a program needn't handle non-finite values. No bound on the sum of `pos_mask` on one device may be relied on, other than what follows from the above.
Results may differ from the reference program's by a relative error of at most 0.0039.
Values may be sent and summed in bfloat16 or wider, within the bound.
No kernel may reach another device: no remote copies, remote signals or barrier semaphores. Data moves between devices by JAX's collectives and lax.ppermute only.
A program may use at most 64 MiB of HBM per device.

```python
import jax
import jax.numpy as jnp
from jax import lax

D = 256
B = 128
NB_DEV = 8
REL_GRP = 4
TILES_DEV = 16
ENTITIES = 524288
RELATIONS = 64
N_GROUP = 16
N_MEMBER = 32


def touch_ends(drawn, key, least, top_value):
    extent = drawn.shape
    spot = [jax.random.randint(jax.random.fold_in(key, axis), (), 0, extent[axis]) for axis in range(len(extent))]
    drawn = drawn.at[tuple(spot)].set(least)
    longest = extent.index(max(extent))
    spot[longest] = (spot[longest] + 1) % extent[longest]
    return drawn.at[tuple(spot)].set(top_value)


def level_of(key, extent, shards, smallest, largest):
    factor_of = 1.0
    for position, parts in shards:
        heights = jax.random.uniform(jax.random.fold_in(jax.random.fold_in(key, 6), position), (parts,), jnp.float32, smallest / len(shards), largest / len(shards))
        factor_of = factor_of * jnp.repeat(jnp.exp(heights), extent[position] // parts).reshape((-1,) + (1,) * (len(extent) - 1 - position))
    return factor_of


def distinct(own_key, rows, number_of, top, lift):
    ranking = jax.random.permutation(jax.random.fold_in(own_key, 1), number_of)
    favour = ranking
    for power in range(3):
        favour = favour * favour // number_of
    favour = favour * lift // number_of
    chance = jax.random.randint(jax.random.fold_in(own_key, 2), (rows, number_of), 0, 4096) + favour
    fixed_rows = jax.random.permutation(jax.random.fold_in(own_key, 3), rows)[jnp.arange(number_of) % rows]
    chance = jnp.where(jnp.arange(rows)[:, None] == fixed_rows[None, :], 1 << 14, chance)
    score = chance * number_of + jnp.arange(number_of)
    return lax.top_k(score.astype(jnp.int32), top)[1].astype(jnp.int32)


def scatter_about(key, extent, width, reach, pieces=(), kind=jnp.bfloat16):
    level = level_of(key, extent, pieces, -0.22, 0.18) if pieces else 1.0
    values = jax.random.normal(key, extent, jnp.float32) * width * level
    return jnp.minimum(jnp.maximum(values, -reach), reach).astype(kind)


def setup_inputs(seed: int = 0) -> dict:
    key_list = jax.random.split(jax.random.key(seed), 9)
    entities = scatter_about(key_list[0], (ENTITIES, D), 0.25, 1.5, ((0, 512),))
    relations = scatter_about(key_list[1], (RELATIONS, D, D), D ** -0.5, 0.375, ((0, 16),))
    src_block = touch_ends(jax.random.randint(key_list[2], (N_GROUP, N_MEMBER, TILES_DEV), 0, NB_DEV), jax.random.fold_in(key_list[2], 1), 0, NB_DEV - 1).astype(jnp.int32)
    dst_member = distinct(key_list[3], N_GROUP * N_MEMBER, N_MEMBER, TILES_DEV, 8192).reshape((N_GROUP, N_MEMBER, TILES_DEV))
    dst_block = touch_ends(jax.random.randint(key_list[4], (N_GROUP, N_MEMBER, TILES_DEV), 0, NB_DEV), jax.random.fold_in(key_list[4], 1), 0, NB_DEV - 1).astype(jnp.int32)
    rel_id = touch_ends(jax.random.randint(key_list[5], (N_GROUP, N_MEMBER, TILES_DEV), 0, REL_GRP), jax.random.fold_in(key_list[5], 1), 0, REL_GRP - 1).astype(jnp.int32)
    neg_block = touch_ends(jax.random.randint(key_list[6], (N_GROUP, N_MEMBER, N_GROUP), 0, NB_DEV), jax.random.fold_in(key_list[6], 1), 0, NB_DEV - 1).astype(jnp.int32)
    pos_mask = touch_ends((jax.random.randint(key_list[7], (N_GROUP, N_MEMBER, TILES_DEV, B, B), 0, 8) < 1).astype(jnp.int32), jax.random.fold_in(key_list[7], 1), 0, 1)
    return {"entities": entities, "relations": relations, "src_block": src_block, "dst_member": dst_member, "dst_block": dst_block, "rel_id": rel_id, "neg_block": neg_block, "pos_mask": pos_mask}


HI = lax.Precision.HIGHEST


def fdot(form, a, b):
    return jnp.einsum(form, a.astype(jnp.float32), b.astype(jnp.float32), precision=HI)


def reference(entities, relations, src_block, dst_member, dst_block, rel_id, neg_block, pos_mask):
    groups = N_GROUP
    members = N_MEMBER
    blocks = entities.reshape(groups, members, NB_DEV, B, D)
    marr = jnp.arange(members, dtype=jnp.int32)[:, None]
    neg_slot = (jnp.arange(TILES_DEV, dtype=jnp.int32) % groups)[None, :]
    rel_group = relations.reshape(groups, REL_GRP, D, D)

    def per_group(grad_acc, g):
        local = blocks[g]
        sb = src_block[g]
        dm = dst_member[g]
        db = dst_block[g]
        src = local[marr, sb]
        dst = local[dm, db]
        nbsel = neg_block[g][:, neg_slot[0]]
        neg = blocks[neg_slot, marr, nbsel]
        rels = rel_group[g][rel_id[g]]
        h = fdot("mkbd,mkde->mkbe", src, rels).astype(jnp.bfloat16)
        pos = fdot("mkbe,mkce->mkbc", h, dst)
        negs = fdot("mkbe,mkce->mkbc", h, neg)
        mask = pos_mask[g].astype(jnp.float32)
        grad_pos = (-mask * jax.nn.sigmoid(-pos)).astype(jnp.bfloat16)
        grad_neg = (0.125 * jax.nn.sigmoid(negs)).astype(jnp.bfloat16)
        grad_h = (fdot("mkbc,mkce->mkbe", grad_pos, dst) + fdot("mkbc,mkce->mkbe", grad_neg, neg)).astype(jnp.bfloat16)
        grad_src = fdot("mkbe,mkde->mkbd", grad_h, rels)
        grad_dst = fdot("mkbc,mkbe->mkce", grad_pos, h)
        grad_negb = fdot("mkbc,mkbe->mkce", grad_neg, h)
        grad_rel = fdot("mkbd,mkbe->mkde", src, grad_h)
        onehot = (rel_id[g][:, :, None] == jnp.arange(REL_GRP, dtype=jnp.int32)[None, None, :]).astype(jnp.float32)
        rel_part = jnp.einsum("mkr,mkde->rde", onehot, grad_rel, precision=HI)
        grad_acc = grad_acc.at[g, marr, sb].add(grad_src)
        grad_acc = grad_acc.at[g, dm, db].add(grad_dst)
        grad_acc = grad_acc.at[neg_slot, marr, nbsel].add(grad_negb)
        return grad_acc, rel_part

    start = jnp.zeros((groups, members, NB_DEV, B, D), jnp.float32)
    grad_acc, rel_parts = lax.scan(per_group, start, jnp.arange(groups, dtype=jnp.int32))
    return grad_acc.reshape(groups * members * NB_DEV * B, D), rel_parts.reshape(groups * REL_GRP, D, D)
```

```python
import jax
import jax.numpy as jnp
from jax import lax
from jax.experimental import pallas as pl
from jax.experimental.pallas import tpu as pltpu
from jax.sharding import PartitionSpec as P

D = 256
B = 128
NB_DEV = 8
TILES = 16
RELS = 4
F32 = jnp.float32
BF16 = jnp.bfloat16

PARAMS = pltpu.CompilerParams(vmem_limit_bytes=24 * 1024 * 1024)
VMEM = pl.BlockSpec(memory_space=pltpu.VMEM)
SMEM = pl.BlockSpec(memory_space=pltpu.SMEM)


def sds(shape, dtype):
    return jax.ShapeDtypeStruct(shape, dtype)


def dot(a, b, dims):
    return lax.dot_general(a, b, (dims, ((), ())), preferred_element_type=F32)


NN = ((1,), (0,))
NT = ((1,), (1,))
TN = ((0,), (0,))


def call(body, ins, outs, flops, nbytes, scratch=(), alias=None):
    return pl.pallas_call(
        body,
        out_shape=outs,
        in_specs=ins,
        out_specs=jax.tree.map(lambda _: VMEM, outs),
        scratch_shapes=scratch,
        compiler_params=PARAMS,
        input_output_aliases=alias or {},
        cost_estimate=pl.CostEstimate(flops=flops, bytes_accessed=nbytes, transcendentals=0),
    )


def pick_body(idx, blocks, *outs):
    n = 0
    for o in outs:
        for t in range(o.shape[0]):
            o[t] = blocks[idx[n]]
            n += 1


def h_body(src, rel, blocks, rels, h):
    for k in range(TILES):
        h[k] = dot(blocks[src[k]], rels[rel[k]], NN).astype(BF16)


def neg_body(tile_of, h, *refs):
    own, sib, gq = refs[:8], refs[8], refs[9]
    outs = refs[10:]
    for s in range(8):
        for t in range(2):
            k = tile_of[2 * s + t]
            neg = own[s][0] if t == 0 else sib[s]
            hk = h[k]
            q = (0.125 * jax.nn.sigmoid(dot(hk, neg, NT))).astype(BF16)
            gq[2 * s + t] = q
            outs[s][t] = dot(q, hk, TN).astype(BF16)


def pos_body(dst, h, received, mask, gp, back):
    for k in range(TILES):
        hk = h[k]
        p = dot(hk, received[dst[k]], NT)
        g = (-mask[k].astype(F32) * jax.nn.sigmoid(-p)).astype(BF16)
        gp[k] = g
        back[dst[k]] = dot(g, hk, TN).astype(BF16)


def own_body(tile_of, dst, src, rel, blocks, rels, received, gp, gq, *refs):
    own, sib, acc, racc = refs[:8], refs[8], refs[9], refs[10]
    acc[...] = jnp.zeros(acc.shape, F32)
    racc[...] = jnp.zeros(racc.shape, F32)
    for s in range(8):
        for t in range(2):
            k = tile_of[2 * s + t]
            neg = own[s][0] if t == 0 else sib[s]
            gh = dot(gp[k], received[dst[k]], NN) + dot(gq[2 * s + t], neg, NN)
            gh = gh.astype(BF16)
            j = src[k]
            r = rel[k]
            acc[j] += dot(gh, rels[r], NT)
            racc[r] += dot(blocks[j], gh, TN)


def add_neg_body(idx, acc_in, *refs):
    own, sib, acc = refs[:8], refs[8], refs[9]
    acc[...] = acc_in[...]
    for s in range(8):
        for t in range(2):
            j = idx[2 * s + t]
            val = own[s][0] if t == 0 else sib[s]
            acc[j] += val.astype(F32)


def add_dst_body(which, wanted, acc_in, back, acc):
    acc[...] = acc_in[...]
    for p in range(back.shape[0]):
        @pl.when(wanted[p] > 0)
        def _():
            j = which[p]
            acc[j] += back[p].astype(F32)


def per_device(entities, relations, src_block, dst_member, dst_block, rel_id, neg_block, pos_mask):
    me = lax.axis_index("member")
    grp = lax.axis_index("group")
    z = grp // 2
    core = grp % 2
    blocks = entities.reshape(NB_DEV, B, D)

    match = dst_member[0] == me
    wanted = jnp.any(match, axis=1).astype(jnp.int32)
    which = jnp.sum(jnp.where(match, dst_block[0], 0), axis=1)
    src = lax.dynamic_index_in_dim(src_block[0], me, 0, keepdims=False)
    dst = lax.dynamic_index_in_dim(dst_member[0], me, 0, keepdims=False)
    rel = lax.dynamic_index_in_dim(rel_id[0], me, 0, keepdims=False)

    outgoing = pick(which, blocks, (32,))[0]
    received = lax.all_to_all(outgoing, "member", split_axis=0, concat_axis=0, tiled=True)

    steps = jnp.arange(8, dtype=jnp.int32)
    sides = jnp.stack([core, 1 - core])
    neg_want = lax.dynamic_index_in_dim(neg_block[:, 0, :], grp, 1, keepdims=False)
    ahead = ((((z + steps) % 8) * 2)[:, None] + sides[None, :]).reshape(16)
    tile_of = ((((z + 8 - steps) % 8) * 2)[:, None] + sides[None, :]).reshape(16)
    ahead_blocks = jnp.take(neg_want, ahead)
    parts = pick(ahead_blocks, blocks, (2,) * 8)
    got = [parts[0]] + [zshift(parts[s], s) for s in range(1, 8)]
    sib = swap(jnp.stack([g[1] for g in got]))

    h = call(h_body, [SMEM, SMEM, VMEM, VMEM], sds((TILES, B, D), BF16), 1 << 28, 2 << 20)(
        src, rel, blocks, relations
    )
    gq, *gn = call(
        neg_body,
        [SMEM] + [VMEM] * 10,
        [sds((TILES, B, B), BF16)] + [sds((2, B, D), BF16)] * 8,
        1 << 28,
        4 << 20,
    )(tile_of, h, *got, sib)
    gp, back = call(
        pos_body,
        [SMEM, VMEM, VMEM, VMEM],
        [sds((TILES, B, B), BF16), sds((32, B, D), BF16)],
        1 << 28,
        6 << 20,
    )(dst, h, received, pos_mask[0, 0])
    back_in = lax.all_to_all(back, "member", split_axis=0, concat_axis=0, tiled=True)

    neg_got = [gn[0]] + [zshift(gn[s], 8 - s) for s in range(1, 8)]
    neg_sib = swap(jnp.stack([g[1] for g in neg_got]))

    acc, racc = call(
        own_body,
        [SMEM] * 4 + [VMEM] * 14,
        [sds((NB_DEV, B, D), F32), sds((RELS, D, D), F32)],
        1 << 29,
        8 << 20,
    )(tile_of, dst, src, rel, blocks, relations, received, gp, gq, *got, sib)

    part = racc.reshape(RELS, 32, 8, D)
    span = 32
    while span > 1:
        span //= 2
        bit = (me // span) % 2
        keep = lax.dynamic_slice_in_dim(part, bit * span, span, 1)
        give = lax.dynamic_slice_in_dim(part, (1 - bit) * span, span, 1)
        part = keep + lax.ppermute(give, "member", [(i, i ^ span) for i in range(32)])
    relation_grad = part.reshape(RELS, 8, D)

    acc = call(
        add_neg_body, [SMEM] + [VMEM] * 10, sds((NB_DEV, B, D), F32), 1 << 20, 3 << 20
    )(ahead_blocks, acc, *neg_got, neg_sib)
    out = call(
        add_dst_body, [SMEM, SMEM, VMEM, VMEM], sds((NB_DEV, B, D), F32), 1 << 20, 4 << 20
    )(which, wanted, acc, back_in)
    return out.reshape(NB_DEV * B, D), relation_grad


def pick(idx, blocks, sizes):
    outs = [sds((n, B, D), BF16) for n in sizes]
    return call(pick_body, [SMEM, VMEM], outs, 0, 3 << 20)(idx, blocks)


def zshift(v, s):
    return lax.ppermute(
        v, "group", [(a * 2 + c, ((a + s) % 8) * 2 + c) for a in range(8) for c in range(2)]
    )


def swap(v):
    return lax.ppermute(v, "group", [(i, i ^ 1) for i in range(16)])


def solution(mesh):
    placed = (
        P(("group", "member"), None),
        P("group", None, None),
        P("group", None, None),
        P("group", None, None),
        P("group", None, None),
        P("group", None, None),
        P(None, "member", None),
        P("group", "member", None, None, None),
    )
    return jax.shard_map(
        per_device,
        mesh=mesh,
        in_specs=placed,
        out_specs=(P(("group", "member"), None), P("group", "member", None)),
        check_vma=False,
    )
```

```python
import jax
import jax.numpy as jnp
from jax import lax
from jax.experimental import pallas as pl
from jax.experimental.pallas import tpu as pltpu
from jax.sharding import PartitionSpec as P

D = 256
B = 128
NB_DEV = 8
TILES = 16
RELS = 4
F32 = jnp.float32
BF16 = jnp.bfloat16

PARAMS = pltpu.CompilerParams(vmem_limit_bytes=24 * 1024 * 1024)
VMEM = pl.BlockSpec(memory_space=pltpu.VMEM)
SMEM = pl.BlockSpec(memory_space=pltpu.SMEM)


def sds(*shape, dtype=BF16):
    return jax.ShapeDtypeStruct(shape, dtype)


def tiles(n):
    return sds(n, B, D)


def dot(a, b, dims):
    return lax.dot_general(a, b, (dims, ((), ())), preferred_element_type=F32)


NN = ((1,), (0,))
NT = ((1,), (1,))
TN = ((0,), (0,))


def call(body, ins, outs, mflops, scratch=(), alias=None):
    return pl.pallas_call(
        body,
        out_shape=outs,
        in_specs=ins,
        out_specs=jax.tree.map(lambda _: VMEM, outs),
        scratch_shapes=scratch,
        compiler_params=PARAMS,
        input_output_aliases=alias or {},
        cost_estimate=pl.CostEstimate(
            flops=mflops << 20, bytes_accessed=4 << 20, transcendentals=0
        ),
    )


def routes(z, c):
    sign = 1 - 2 * c

    def at(dz, core):
        return ((z + dz + 8) % 8) * 2 + core

    give, keep, org = [at(0, 1 - c)], [], [at(0, c), at(0, 1 - c)]
    for j in (1, 2, 3):
        give += [at(-sign * j, 1 - c), at(-sign * j, c)]
        keep += [at(sign * j, c), at(sign * j, 1 - c)]
        org += [at(-sign * j, c), at(-sign * j, 1 - c)]
    far = [at(4, c), at(4, 1 - c)]
    org += far[:1]
    for j in (1, 2, 3):
        org += [at(sign * j, 1 - c), at(sign * j, c)]
    return jnp.stack(give + keep + far + [at(0, c)]), jnp.stack(org + far[1:])


PLACE = (15, 0, 2, 1, 4, 3, 6, 5, 13, 8, 7, 10, 9, 12, 11, 14)


def swap(v):
    return lax.ppermute(v, "group", [(i, i ^ 1) for i in range(16)])


def zmove(v, j):
    pairs = []
    for a in range(8):
        pairs += [(a * 2, ((a + j) % 8) * 2), (a * 2 + 1, ((a - j) % 8) * 2 + 1)]
    return lax.ppermute(v, "group", pairs)


def mix_body(own, arrived, *outs):
    for j in range(3):
        outs[j][0] = own[2 * j]
        outs[j][1] = own[2 * j + 1]
        outs[j][2] = arrived[1 + 2 * j]
        outs[j][3] = arrived[2 + 2 * j]


def pack_body(arrived, r1, r2, r3, r4, packed, mine):
    mine[0] = arrived[0]
    for j, r in enumerate((r1, r2, r3)):
        packed[2 * j] = r[1]
        packed[2 * j + 1] = r[3]
        mine[1 + 2 * j] = r[0]
        mine[2 + 2 * j] = r[2]
    packed[6] = r4[1]
    mine[7] = r4[0]


def exchange(give, own, far):
    arrived = swap(give)
    sends = call(mix_body, [VMEM] * 2, [tiles(4)] * 3, 0)(own, arrived)
    got = [zmove(v, j + 1) for j, v in enumerate(sends)] + [zmove(far, 4)]
    packed, mine = call(pack_body, [VMEM] * 5, [tiles(7), tiles(8)], 0)(arrived, *got)
    return mine, swap(packed)


def slots(mine, last):
    return [(mine, i) for i in range(8)] + [(last, i) for i in range(7)]


ASKED, ORG, SRC, DST, REL, ORDER = (16 * i for i in range(6))


def pick_body(idx, blocks, out):
    for p in range(32):
        out[p] = blocks[idx[p]]


def pre_body(idx, blocks, give, own, far):
    n = 0
    for out in (give, own, far):
        for i in range(out.shape[0]):
            out[i] = blocks[idx[ASKED + idx[ORDER + n]]]
            n += 1


def tile_body(idx, blocks, rels, received, mask, mine, last, back, acc, gn, racc):
    acc[...] = jnp.zeros(acc.shape, F32)
    racc[...] = jnp.zeros(racc.shape, F32)
    stays = (blocks, idx[ASKED + idx[ORG]])
    for i, (ref, at) in enumerate([stays] + slots(mine, last)):
        k = idx[ORG + i]
        j, r, d = idx[SRC + k], idx[REL + k], idx[DST + k]
        own, op = blocks[j], rels[r]
        h = dot(own, op, NN).astype(BF16)
        both = jnp.concatenate([received[d], ref[at]], axis=0)
        scores = dot(h, both, NT)
        gp = -mask[k].astype(F32) * jax.nn.sigmoid(-scores[:, :B])
        gq = 0.125 * jax.nn.sigmoid(scores[:, B:])
        g = jnp.concatenate([gp, gq], axis=1).astype(BF16)
        gb = dot(g, h, TN).astype(BF16)
        back[d, :B] = gb[:B]
        gn[PLACE[i]] = gb[B:]
        gh = dot(g, both, NN).astype(BF16)
        acc[j] += dot(gh, op, NT)
        racc[r] += dot(own, gh, TN)
    for p in range(32):
        rows = [racc[r, 8 * p : 8 * p + 8] for r in range(RELS)]
        back[p, B:] = jnp.concatenate(rows, axis=0).astype(BF16)


def add_neg_body(idx, acc_in, gn, mine, last, acc):
    for i, (ref, at) in enumerate([(gn, 15)] + slots(mine, last)):
        acc[idx[ASKED + idx[ORG + i]]] += ref[at].astype(F32)


def add_dst_body(which, wanted, acc_in, back, acc, rel_out):
    rel_out[...] = jnp.zeros(rel_out.shape, F32)
    for p in range(32):
        rel_out[...] += back[p, B:].astype(F32)

        @pl.when(wanted[p] > 0)
        def _():
            acc[which[p]] += back[p, :B].astype(F32)


def per_device(entities, relations, src_block, dst_member, dst_block, rel_id, neg_block, pos_mask):
    me = lax.axis_index("member")
    grp = lax.axis_index("group")
    blocks = entities.reshape(NB_DEV, B, D)
    mask = pos_mask[0, 0]

    match = dst_member[0] == me
    wanted = jnp.any(match, axis=1).astype(jnp.int32)
    which = jnp.sum(jnp.where(match, dst_block[0], 0), axis=1)
    outgoing = call(pick_body, [SMEM, VMEM], tiles(32), 0)(which, blocks)
    received = lax.all_to_all(outgoing, "member", split_axis=0, concat_axis=0, tiled=True)

    src = lax.dynamic_index_in_dim(src_block[0], me, 0, keepdims=False)
    dst = lax.dynamic_index_in_dim(dst_member[0], me, 0, keepdims=False)
    rel = lax.dynamic_index_in_dim(rel_id[0], me, 0, keepdims=False)
    asked = lax.dynamic_index_in_dim(neg_block[:, 0, :], grp, 1, keepdims=False)
    order, org = routes(grp // 2, grp % 2)
    idx = jnp.concatenate([asked, org, src, dst, rel, order])

    sends = call(pre_body, [SMEM, VMEM], [tiles(7), tiles(6), tiles(2)], 0)(idx, blocks)
    mine, last = exchange(*sends)
    sums = sds(NB_DEV, B, D, dtype=F32)
    back, acc, gn = call(
        tile_body,
        [SMEM] + [VMEM] * 6,
        [sds(32, B + RELS * 8, D), sums, tiles(TILES)],
        1600,
        [pltpu.VMEM((RELS, D, D), F32)],
    )(idx, blocks, relations, received, mask, mine, last)
    back_in = lax.all_to_all(back, "member", split_axis=0, concat_axis=0, tiled=True)

    mine, last = exchange(gn[:7], gn[7:13], gn[13:15])
    acc = call(add_neg_body, [SMEM] + [VMEM] * 4, sums, 1, alias={1: 0})(
        idx, acc, gn, mine, last
    )
    back_in, acc = lax.optimization_barrier((back_in, acc))
    out, relation_grad = call(
        add_dst_body,
        [SMEM] * 2 + [VMEM] * 2,
        [sums, sds(RELS * 8, D, dtype=F32)],
        1,
        alias={2: 0},
    )(which, wanted, acc, back_in)
    return out.reshape(NB_DEV * B, D), relation_grad.reshape(RELS, 8, D)


def solution(mesh):
    placed = (
        P(("group", "member"), None),
        P("group", None, None),
        P("group", None, None),
        P("group", None, None),
        P("group", None, None),
        P("group", None, None),
        P(None, "member", None),
        P("group", "member", None, None, None),
    )
    return jax.shard_map(
        per_device,
        mesh=mesh,
        in_specs=placed,
        out_specs=(P(("group", "member"), None), P("group", "member", None)),
        check_vma=False,
    )
```

```python
import jax
import jax.numpy as jnp
from jax import lax
from jax.experimental import pallas as pl
from jax.experimental.pallas import tpu as pltpu
from jax.sharding import PartitionSpec as P

D = 256
B = 128
NB_DEV = 8
TILES = 16
RELS = 4
F32 = jnp.float32
BF16 = jnp.bfloat16

PARAMS = pltpu.CompilerParams(vmem_limit_bytes=24 * 1024 * 1024)
VMEM = pl.BlockSpec(memory_space=pltpu.VMEM)
SMEM = pl.BlockSpec(memory_space=pltpu.SMEM)


def sds(*shape, dtype=BF16):
    return jax.ShapeDtypeStruct(shape, dtype)


def tiles(n):
    return sds(n, B, D)


def dot(a, b, dims):
    return lax.dot_general(a, b, (dims, ((), ())), preferred_element_type=F32)


NN = ((1,), (0,))
NT = ((1,), (1,))
TN = ((0,), (0,))


def call(body, ins, outs, mflops, scratch=()):
    return pl.pallas_call(
        body,
        out_shape=outs,
        in_specs=ins,
        out_specs=jax.tree.map(lambda _: VMEM, outs),
        scratch_shapes=scratch,
        compiler_params=PARAMS,
        cost_estimate=pl.CostEstimate(
            flops=mflops << 20, bytes_accessed=4 << 20, transcendentals=0
        ),
    )


def routes(z, c):
    sign = 1 - 2 * c

    def at(dz, core):
        return ((z + dz + 8) % 8) * 2 + core

    give, keep, org = [at(0, 1 - c)], [], [at(0, c), at(0, 1 - c)]
    for j in (1, 2, 3):
        give += [at(-sign * j, 1 - c), at(-sign * j, c)]
        keep += [at(sign * j, c), at(sign * j, 1 - c)]
        org += [at(-sign * j, c), at(-sign * j, 1 - c)]
    far = [at(4, c), at(4, 1 - c)]
    org += far[:1]
    for j in (1, 2, 3):
        org += [at(sign * j, 1 - c), at(sign * j, c)]
    return jnp.stack(give + keep + far + [at(0, c)]), jnp.stack(org + far[1:])


PLACE = (15, 0, 2, 1, 4, 3, 6, 5, 13, 8, 7, 10, 9, 12, 11, 14)


def swap(v):
    return lax.ppermute(v, "group", [(i, i ^ 1) for i in range(16)])


def zmove(v, j):
    pairs = []
    for a in range(8):
        pairs += [(a * 2, ((a + j) % 8) * 2), (a * 2 + 1, ((a - j) % 8) * 2 + 1)]
    return lax.ppermute(v, "group", pairs)


def mix_body(own, arrived, *outs):
    for j in range(3):
        outs[j][0] = own[2 * j]
        outs[j][1] = own[2 * j + 1]
        outs[j][2] = arrived[1 + 2 * j]
        outs[j][3] = arrived[2 + 2 * j]


def pack_body(arrived, r1, r2, r3, r4, packed, mine):
    mine[0] = arrived[0]
    for j, r in enumerate((r1, r2, r3)):
        packed[2 * j] = r[1]
        packed[2 * j + 1] = r[3]
        mine[1 + 2 * j] = r[0]
        mine[2 + 2 * j] = r[2]
    packed[6] = r4[1]
    mine[7] = r4[0]


def exchange(give, own, far):
    arrived = swap(give)
    sends = call(mix_body, [VMEM] * 2, [tiles(4)] * 3, 0)(own, arrived)
    got = [zmove(v, j + 1) for j, v in enumerate(sends)] + [zmove(far, 4)]
    packed, mine = call(pack_body, [VMEM] * 5, [tiles(7), tiles(8)], 0)(arrived, *got)
    return mine, swap(packed)


def slots(mine, last):
    return [(mine, i) for i in range(8)] + [(last, i) for i in range(7)]


ASKED, ORG, SRC, DST, REL, ORDER = (16 * i for i in range(6))


def pick_body(code, blocks, out):
    for p in range(32):
        out[p] = blocks[jnp.maximum(code[p] - 1, 0)]


def pre_body(idx, blocks, give, own, far):
    n = 0
    for out in (give, own, far):
        for i in range(out.shape[0]):
            out[i] = blocks[idx[ASKED + idx[ORDER + n]]]
            n += 1


def stage_body(idx, blocks, rels, mask, mine, last, stage, h_v):
    stays = (blocks, idx[ASKED + idx[ORG]])
    work = []
    for i, (ref, at) in enumerate([stays] + slots(mine, last)):
        k = idx[ORG + i]
        work.append((i, k, idx[SRC + k], idx[REL + k], ref, at))
    for i, k, j, r, ref, at in work:
        h_v[i] = dot(blocks[j], rels[r], NN).astype(BF16)
    for i, k, j, r, ref, at in work:
        neg = ref[at]
        stage[i] = neg
        gq = 0.125 * jax.nn.sigmoid(dot(h_v[i], neg, NT))
        pair = [mask[k].astype(F32), gq]
        stage[TILES + i] = jnp.concatenate(pair, axis=1).astype(BF16)


def tile_body(idx, blocks, rels, received, stage, back, acc, racc, h_v, g_v, gh_v):
    work = []
    for i in range(TILES):
        k = idx[ORG + i]
        work.append((i, idx[SRC + k], idx[REL + k], idx[DST + k]))
    acc[...] = jnp.zeros(acc.shape, F32)
    racc[...] = jnp.zeros(racc.shape, F32)
    for i, j, r, d in work:
        h_v[i] = dot(blocks[j], rels[r], NN).astype(BF16)
    for i, j, r, d in work:
        mask = stage[TILES + i, :, :B].astype(F32)
        gp = -mask * jax.nn.sigmoid(-dot(h_v[i], received[d], NT))
        g_v[i, :, :B] = gp.astype(BF16)
        g_v[i, :, B:] = stage[TILES + i, :, B:]
    for i, j, r, d in work:
        both = jnp.concatenate([received[d], stage[i]], axis=0)
        gh_v[i] = dot(g_v[i], both, NN).astype(BF16)
    for i, j, r, d in work:
        back[d, :B] = dot(g_v[i, :, :B], h_v[i], TN).astype(BF16)
    for i, j, r, d in work:
        racc[r] += dot(blocks[j], gh_v[i], TN)
        acc[j] += dot(gh_v[i], rels[r], NT)
    for p in range(32):
        rows = [racc[r, 8 * p : 8 * p + 8] for r in range(RELS)]
        back[p, B:] = jnp.concatenate(rows, axis=0).astype(BF16)


def neg_body(idx, blocks, rels, stage, give, own, far, stays, h_v):
    for i in range(TILES):
        k = idx[ORG + i]
        h_v[i] = dot(blocks[idx[SRC + k]], rels[idx[REL + k]], NN).astype(BF16)
    outs = [(ref, at) for ref in (give, own, far, stays) for at in range(ref.shape[0])]
    for i in range(TILES):
        ref, at = outs[PLACE[i]]
        ref[at] = dot(stage[TILES + i, :, B:], h_v[i], TN).astype(BF16)


def add_neg_body(idx, acc_in, stays, mine, last, acc):
    acc[...] = acc_in[...]
    for i, (ref, at) in enumerate([(stays, 0)] + slots(mine, last)):
        acc[idx[ASKED + idx[ORG + i]]] += ref[at].astype(F32)


def add_dst_body(code, acc_in, back, acc, rel_out):
    acc[...] = acc_in[...]
    rel_out[...] = jnp.zeros(rel_out.shape, F32)
    for p in range(32):
        rel_out[...] += back[p, B:].astype(F32)

        @pl.when(code[p] > 0)
        def _():
            acc[code[p] - 1] += back[p, :B].astype(F32)


def per_device(entities, relations, src_block, dst_member, dst_block, rel_id, neg_block, pos_mask):
    me = lax.axis_index("member")
    grp = lax.axis_index("group")
    blocks = entities.reshape(NB_DEV, B, D)
    mask = pos_mask[0, 0]

    match = dst_member[0] == me
    code = jnp.sum(jnp.where(match, dst_block[0] + 1, 0), axis=1)
    outgoing = call(pick_body, [SMEM, VMEM], tiles(32), 0)(code, blocks)
    received = lax.all_to_all(outgoing, "member", split_axis=0, concat_axis=0, tiled=True)

    src = lax.dynamic_index_in_dim(src_block[0], me, 0, keepdims=False)
    dst = lax.dynamic_index_in_dim(dst_member[0], me, 0, keepdims=False)
    rel = lax.dynamic_index_in_dim(rel_id[0], me, 0, keepdims=False)
    asked = lax.dynamic_index_in_dim(neg_block[:, 0, :], grp, 1, keepdims=False)
    order, org = routes(grp // 2, grp % 2)
    idx = jnp.concatenate([asked, org, src, dst, rel, order])

    sends = call(pre_body, [SMEM, VMEM], [tiles(7), tiles(6), tiles(2)], 0)(idx, blocks)
    mine, last = exchange(*sends)
    sums = sds(NB_DEV, B, D, dtype=F32)
    tile_store = pltpu.VMEM((TILES, B, D), BF16)
    stage = call(stage_body, [SMEM] + [VMEM] * 5, tiles(TILES * 2), 256, [tile_store])(
        idx, blocks, relations, mask, mine, last
    )
    back, acc = call(
        tile_body,
        [SMEM] + [VMEM] * 4,
        [sds(32, B + RELS * 8, D), sums],
        1600,
        [pltpu.VMEM((RELS, D, D), F32)] + [tile_store] * 3,
    )(idx, blocks, relations, received, stage)
    back, stage = lax.optimization_barrier((back, stage))
    back_in = lax.all_to_all(back, "member", split_axis=0, concat_axis=0, tiled=True)

    give, own, far, stays = call(
        neg_body,
        [SMEM] + [VMEM] * 3,
        [tiles(7), tiles(6), tiles(2), tiles(1)],
        512,
        [tile_store],
    )(idx, blocks, relations, stage)
    mine, last = exchange(give, own, far)
    acc = call(add_neg_body, [SMEM] + [VMEM] * 4, sums, 1)(
        idx, acc, stays, mine, last
    )
    back_in, acc = lax.optimization_barrier((back_in, acc))
    out, relation_grad = call(
        add_dst_body,
        [SMEM] + [VMEM] * 2,
        [sums, sds(RELS * 8, D, dtype=F32)],
        1,
    )(code, acc, back_in)
    return out.reshape(NB_DEV * B, D), relation_grad.reshape(RELS, 8, D)


def solution(mesh):
    placed = (
        P(("group", "member"), None),
        P("group", None, None),
        P("group", None, None),
        P("group", None, None),
        P("group", None, None),
        P("group", None, None),
        P(None, "member", None),
        P("group", "member", None, None, None),
    )
    return jax.shard_map(
        per_device,
        mesh=mesh,
        in_specs=placed,
        out_specs=(P(("group", "member"), None), P("group", "member", None)),
        check_vma=False,
    )
```

```python
import jax
import jax.numpy as jnp
from jax import lax
from jax.experimental import pallas as pl
from jax.experimental.pallas import tpu as pltpu
from jax.sharding import PartitionSpec as P

D = 256
B = 128
NB_DEV = 8
TILES = 16
RELS = 4
F32 = jnp.float32
BF16 = jnp.bfloat16

PARAMS = pltpu.CompilerParams(vmem_limit_bytes=24 * 1024 * 1024)
VMEM = pl.BlockSpec(memory_space=pltpu.VMEM)
SMEM = pl.BlockSpec(memory_space=pltpu.SMEM)


def sds(*shape, dtype=BF16):
    return jax.ShapeDtypeStruct(shape, dtype)


def tiles(n):
    return sds(n, B, D)


def dot(a, b, dims):
    return lax.dot_general(a, b, (dims, ((), ())), preferred_element_type=F32)


NN = ((1,), (0,))
NT = ((1,), (1,))
TN = ((0,), (0,))


def call(body, ins, outs, mflops, scratch=()):
    return pl.pallas_call(
        body,
        out_shape=outs,
        in_specs=ins,
        out_specs=jax.tree.map(lambda _: VMEM, outs),
        scratch_shapes=scratch,
        compiler_params=PARAMS,
        cost_estimate=pl.CostEstimate(
            flops=mflops << 20, bytes_accessed=4 << 20, transcendentals=0
        ),
    )


def routes(z, c):
    sign = 1 - 2 * c

    def at(dz, core):
        return ((z + dz + 8) % 8) * 2 + core

    give, keep, org = [at(0, 1 - c)], [], [at(0, c), at(0, 1 - c)]
    for j in (1, 2, 3):
        give += [at(-sign * j, 1 - c), at(-sign * j, c)]
        keep += [at(sign * j, c), at(sign * j, 1 - c)]
        org += [at(-sign * j, c), at(-sign * j, 1 - c)]
    far = [at(4, c), at(4, 1 - c)]
    org += far[:1]
    for j in (1, 2, 3):
        org += [at(sign * j, 1 - c), at(sign * j, c)]
    return jnp.stack(give + keep + far + [at(0, c)]), jnp.stack(org + far[1:])


PLACE = (15, 0, 2, 1, 4, 3, 6, 5, 13, 8, 7, 10, 9, 12, 11, 14)


def swap(v):
    return lax.ppermute(v, "group", [(i, i ^ 1) for i in range(16)])


def zmove(v, j):
    pairs = []
    for a in range(8):
        pairs += [(a * 2, ((a + j) % 8) * 2), (a * 2 + 1, ((a - j) % 8) * 2 + 1)]
    return lax.ppermute(v, "group", pairs)


def mix_body(own, arrived, *outs):
    for j in range(3):
        outs[j][0] = own[2 * j]
        outs[j][1] = own[2 * j + 1]
        outs[j][2] = arrived[1 + 2 * j]
        outs[j][3] = arrived[2 + 2 * j]


def pack_body(arrived, r1, r2, r3, r4, packed, mine):
    mine[0] = arrived[0]
    for j, r in enumerate((r1, r2, r3)):
        packed[2 * j] = r[1]
        packed[2 * j + 1] = r[3]
        mine[1 + 2 * j] = r[0]
        mine[2 + 2 * j] = r[2]
    packed[6] = r4[1]
    mine[7] = r4[0]


def exchange(give, own, far):
    arrived = swap(give)
    sends = call(mix_body, [VMEM] * 2, [tiles(4)] * 3, 0)(own, arrived)
    got = [zmove(v, j + 1) for j, v in enumerate(sends)] + [zmove(far, 4)]
    packed, mine = call(pack_body, [VMEM] * 5, [tiles(7), tiles(8)], 0)(arrived, *got)
    return mine, swap(packed)


def slots(mine, last):
    return [(mine, i) for i in range(8)] + [(last, i) for i in range(7)]


ASKED, ORG, SRC, DST, REL, ORDER = (16 * i for i in range(6))


def pick_body(code, blocks, out):
    for p in range(32):
        out[p] = blocks[jnp.maximum(code[p] - 1, 0)]


def pre_body(idx, blocks, give, own, far):
    n = 0
    for out in (give, own, far):
        for i in range(out.shape[0]):
            out[i] = blocks[idx[ASKED + idx[ORDER + n]]]
            n += 1


def stage_body(idx, blocks, rels, mask, mine, last, stage, h_v):
    stays = (blocks, idx[ASKED + idx[ORG]])
    work = []
    for i, (ref, at) in enumerate([stays] + slots(mine, last)):
        k = idx[ORG + i]
        work.append((i, k, idx[SRC + k], idx[REL + k], ref, at))
    for i, k, j, r, ref, at in work:
        h_v[i] = dot(blocks[j], rels[r], NN).astype(BF16)
    for i, k, j, r, ref, at in work:
        neg = ref[at]
        stage[i] = neg
        gq = 0.125 * jax.nn.sigmoid(dot(h_v[i], neg, NT))
        pair = [mask[k].astype(F32), gq]
        stage[TILES + i] = jnp.concatenate(pair, axis=1).astype(BF16)


def tile_body(idx, blocks, rels, received, stage, back, gh_v, racc, h_v, g_v):
    work = []
    for i in range(TILES):
        k = idx[ORG + i]
        work.append((i, idx[SRC + k], idx[REL + k], idx[DST + k]))
    racc[...] = jnp.zeros(racc.shape, F32)
    for i, j, r, d in work:
        h_v[i] = dot(blocks[j], rels[r], NN).astype(BF16)
    for i, j, r, d in work:
        mask = stage[TILES + i, :, :B].astype(F32)
        gp = -mask * jax.nn.sigmoid(-dot(h_v[i], received[d], NT))
        g_v[i, :, :B] = gp.astype(BF16)
        g_v[i, :, B:] = stage[TILES + i, :, B:]
    for i, j, r, d in work:
        both = jnp.concatenate([received[d], stage[i]], axis=0)
        gh_v[i] = dot(g_v[i], both, NN).astype(BF16)
    for i, j, r, d in work:
        back[d, :B] = dot(g_v[i, :, :B], h_v[i], TN).astype(BF16)
    for i, j, r, d in work:
        racc[r] += dot(blocks[j], gh_v[i], TN)
    for p in range(32):
        rows = [racc[r, 8 * p : 8 * p + 8] for r in range(RELS)]
        back[p, B:] = jnp.concatenate(rows, axis=0).astype(BF16)


def neg_body(idx, blocks, rels, stage, give, own, far, stays, h_v):
    for i in range(TILES):
        k = idx[ORG + i]
        h_v[i] = dot(blocks[idx[SRC + k]], rels[idx[REL + k]], NN).astype(BF16)
    outs = [(ref, at) for ref in (give, own, far, stays) for at in range(ref.shape[0])]
    for i in range(TILES):
        ref, at = outs[PLACE[i]]
        ref[at] = dot(stage[TILES + i, :, B:], h_v[i], TN).astype(BF16)


def add_neg_body(idx, rels, gh, stays, mine, last, acc):
    acc[...] = jnp.zeros(acc.shape, F32)
    for i in range(TILES):
        k = idx[ORG + i]
        acc[idx[SRC + k]] += dot(gh[i], rels[idx[REL + k]], NT)
    for i, (ref, at) in enumerate([(stays, 0)] + slots(mine, last)):
        acc[idx[ASKED + idx[ORG + i]]] += ref[at].astype(F32)


def add_dst_body(code, acc_in, back, acc, rel_out):
    acc[...] = acc_in[...]
    rel_out[...] = jnp.zeros(rel_out.shape, F32)
    for p in range(32):
        rel_out[...] += back[p, B:].astype(F32)

        @pl.when(code[p] > 0)
        def _():
            acc[code[p] - 1] += back[p, :B].astype(F32)


def per_device(entities, relations, src_block, dst_member, dst_block, rel_id, neg_block, pos_mask):
    me = lax.axis_index("member")
    grp = lax.axis_index("group")
    blocks = entities.reshape(NB_DEV, B, D)
    mask = pos_mask[0, 0]

    match = dst_member[0] == me
    code = jnp.sum(jnp.where(match, dst_block[0] + 1, 0), axis=1)
    outgoing = call(pick_body, [SMEM, VMEM], tiles(32), 0)(code, blocks)
    received = lax.all_to_all(outgoing, "member", split_axis=0, concat_axis=0, tiled=True)

    src = lax.dynamic_index_in_dim(src_block[0], me, 0, keepdims=False)
    dst = lax.dynamic_index_in_dim(dst_member[0], me, 0, keepdims=False)
    rel = lax.dynamic_index_in_dim(rel_id[0], me, 0, keepdims=False)
    asked = lax.dynamic_index_in_dim(neg_block[:, 0, :], grp, 1, keepdims=False)
    order, org = routes(grp // 2, grp % 2)
    idx = jnp.concatenate([asked, org, src, dst, rel, order])

    sends = call(pre_body, [SMEM, VMEM], [tiles(7), tiles(6), tiles(2)], 0)(idx, blocks)
    mine, last = exchange(*sends)
    sums = sds(NB_DEV, B, D, dtype=F32)
    tile_store = pltpu.VMEM((TILES, B, D), BF16)
    stage = call(stage_body, [SMEM] + [VMEM] * 5, tiles(TILES * 2), 256, [tile_store])(
        idx, blocks, relations, mask, mine, last
    )
    back, gh = call(
        tile_body,
        [SMEM] + [VMEM] * 4,
        [sds(32, B + RELS * 8, D), tiles(TILES)],
        1600,
        [pltpu.VMEM((RELS, D, D), F32)] + [tile_store] * 2,
    )(idx, blocks, relations, received, stage)
    back, stage = lax.optimization_barrier((back, stage))
    back_in = lax.all_to_all(back, "member", split_axis=0, concat_axis=0, tiled=True)

    give, own, far, stays = call(
        neg_body,
        [SMEM] + [VMEM] * 3,
        [tiles(7), tiles(6), tiles(2), tiles(1)],
        512,
        [tile_store],
    )(idx, blocks, relations, stage)
    mine, last = exchange(give, own, far)
    acc = call(add_neg_body, [SMEM] + [VMEM] * 5, sums, 256)(
        idx, relations, gh, stays, mine, last
    )
    back_in, acc = lax.optimization_barrier((back_in, acc))
    out, relation_grad = call(
        add_dst_body,
        [SMEM] + [VMEM] * 2,
        [sums, sds(RELS * 8, D, dtype=F32)],
        1,
    )(code, acc, back_in)
    return out.reshape(NB_DEV * B, D), relation_grad.reshape(RELS, 8, D)


def solution(mesh):
    placed = (
        P(("group", "member"), None),
        P("group", None, None),
        P("group", None, None),
        P("group", None, None),
        P("group", None, None),
        P("group", None, None),
        P(None, "member", None),
        P("group", "member", None, None, None),
    )
    return jax.shard_map(
        per_device,
        mesh=mesh,
        in_specs=placed,
        out_specs=(P(("group", "member"), None), P("group", "member", None)),
        check_vma=False,
    )
```

```python
import jax
import jax.numpy as jnp
from jax import lax
from jax.experimental import pallas as pl
from jax.experimental.pallas import tpu as pltpu
from jax.sharding import PartitionSpec as P

D = 256
B = 128
NB_DEV = 8
TILES = 16
RELS = 4
F32 = jnp.float32
BF16 = jnp.bfloat16

PARAMS = pltpu.CompilerParams(vmem_limit_bytes=24 * 1024 * 1024)
VMEM = pl.BlockSpec(memory_space=pltpu.VMEM)
SMEM = pl.BlockSpec(memory_space=pltpu.SMEM)


def sds(*shape, dtype=BF16):
    return jax.ShapeDtypeStruct(shape, dtype)


def tiles(n):
    return sds(n, B, D)


def dot(a, b, dims):
    return lax.dot_general(a, b, (dims, ((), ())), preferred_element_type=F32)


NN = ((1,), (0,))
NT = ((1,), (1,))
TN = ((0,), (0,))


def call(body, ins, outs, mflops, scratch=()):
    return pl.pallas_call(
        body,
        out_shape=outs,
        in_specs=ins,
        out_specs=jax.tree.map(lambda _: VMEM, outs),
        scratch_shapes=scratch,
        compiler_params=PARAMS,
        cost_estimate=pl.CostEstimate(
            flops=mflops << 20, bytes_accessed=4 << 20, transcendentals=0
        ),
    )


def routes(z, c):
    sign = 1 - 2 * c

    def at(dz, core):
        return ((z + dz + 8) % 8) * 2 + core

    give, keep, org = [at(0, 1 - c)], [], [at(0, c), at(0, 1 - c)]
    for j in (1, 2, 3):
        give += [at(-sign * j, 1 - c), at(-sign * j, c)]
        keep += [at(sign * j, c), at(sign * j, 1 - c)]
        org += [at(-sign * j, c), at(-sign * j, 1 - c)]
    far = [at(4, c), at(4, 1 - c)]
    org += far[:1]
    for j in (1, 2, 3):
        org += [at(sign * j, 1 - c), at(sign * j, c)]
    return jnp.stack(give + keep + far + [at(0, c)]), jnp.stack(org + far[1:])


PLACE = (15, 0, 2, 1, 4, 3, 6, 5, 13, 8, 7, 10, 9, 12, 11, 14)


def swap(v):
    return lax.ppermute(v, "group", [(i, i ^ 1) for i in range(16)])


def zmove(v, j):
    pairs = []
    for a in range(8):
        pairs += [(a * 2, ((a + j) % 8) * 2), (a * 2 + 1, ((a - j) % 8) * 2 + 1)]
    return lax.ppermute(v, "group", pairs)


def mix_body(own, arrived, *outs):
    for j in range(3):
        outs[j][0] = own[2 * j]
        outs[j][1] = own[2 * j + 1]
        outs[j][2] = arrived[1 + 2 * j]
        outs[j][3] = arrived[2 + 2 * j]


def pack_body(arrived, r1, r2, r3, r4, packed, mine):
    mine[0] = arrived[0]
    for j, r in enumerate((r1, r2, r3)):
        packed[2 * j] = r[1]
        packed[2 * j + 1] = r[3]
        mine[1 + 2 * j] = r[0]
        mine[2 + 2 * j] = r[2]
    packed[6] = r4[1]
    mine[7] = r4[0]


def exchange(give, own, far):
    arrived = swap(give)
    sends = call(mix_body, [VMEM] * 2, [tiles(4)] * 3, 0)(own, arrived)
    got = [zmove(v, j + 1) for j, v in enumerate(sends)] + [zmove(far, 4)]
    packed, mine = call(pack_body, [VMEM] * 5, [tiles(7), tiles(8)], 0)(arrived, *got)
    return mine, swap(packed)


def slots(mine, last):
    return [(mine, i) for i in range(8)] + [(last, i) for i in range(7)]


ASKED, ORG, SRC, DST, REL, ORDER = (16 * i for i in range(6))


def pick_body(code, blocks, out):
    for p in range(32):
        out[p] = blocks[jnp.maximum(code[p] - 1, 0)]


def pre_body(idx, blocks, give, own, far):
    n = 0
    for out in (give, own, far):
        for i in range(out.shape[0]):
            out[i] = blocks[idx[ASKED + idx[ORDER + n]]]
            n += 1


def stage_body(idx, blocks, rels, mask, mine, last, stage, h_v):
    stays = (blocks, idx[ASKED + idx[ORG]])
    work = []
    for i, (ref, at) in enumerate([stays] + slots(mine, last)):
        k = idx[ORG + i]
        work.append((i, k, idx[SRC + k], idx[REL + k], ref, at))
    for i, k, j, r, ref, at in work:
        h_v[i] = dot(blocks[j], rels[r], NN).astype(BF16)
    for i, k, j, r, ref, at in work:
        neg = ref[at]
        stage[i] = neg
        gq = 0.125 * jax.nn.sigmoid(dot(h_v[i], neg, NT))
        pair = [mask[k].astype(F32), gq]
        stage[TILES + i] = jnp.concatenate(pair, axis=1).astype(BF16)


def tile_body(idx, blocks, rels, received, stage, back, gh_v, racc, h_v, g_v):
    work = []
    for i in range(TILES):
        k = idx[ORG + i]
        work.append((i, idx[SRC + k], idx[REL + k], idx[DST + k]))
    racc[...] = jnp.zeros(racc.shape, F32)
    for i, j, r, d in work:
        h_v[i] = dot(blocks[j], rels[r], NN).astype(BF16)
    for i, j, r, d in work:
        mask = stage[TILES + i, :, :B].astype(F32)
        gp = -mask * jax.nn.sigmoid(-dot(h_v[i], received[d], NT))
        g_v[i, :, :B] = gp.astype(BF16)
        g_v[i, :, B:] = stage[TILES + i, :, B:]
    for i, j, r, d in work:
        both = jnp.concatenate([received[d], stage[i]], axis=0)
        gh_v[i] = dot(g_v[i], both, NN).astype(BF16)
    for i, j, r, d in work:
        back[d, :B] = dot(g_v[i, :, :B], h_v[i], TN).astype(BF16)
    for i, j, r, d in work:
        racc[r] += dot(blocks[j], gh_v[i], TN)
    for p in range(32):
        rows = [racc[r, 8 * p : 8 * p + 8] for r in range(RELS)]
        back[p, B:] = jnp.concatenate(rows, axis=0).astype(BF16)


def neg_body(idx, blocks, rels, stage, give, own, far, stays, h_v):
    for i in range(TILES):
        k = idx[ORG + i]
        h_v[i] = dot(blocks[idx[SRC + k]], rels[idx[REL + k]], NN).astype(BF16)
    outs = [(ref, at) for ref in (give, own, far, stays) for at in range(ref.shape[0])]
    for i in range(TILES):
        ref, at = outs[PLACE[i]]
        ref[at] = dot(stage[TILES + i, :, B:], h_v[i], TN).astype(BF16)


def add_neg_body(idx, rels, gh, stays, mine, last, acc):
    acc[...] = jnp.zeros(acc.shape, F32)
    for i in range(TILES):
        k = idx[ORG + i]
        acc[idx[SRC + k]] += dot(gh[i], rels[idx[REL + k]], NT)
    for i, (ref, at) in enumerate([(stays, 0)] + slots(mine, last)):
        acc[idx[ASKED + idx[ORG + i]]] += ref[at].astype(F32)


def add_dst_body(code, acc_in, back, acc, rel_out):
    acc[...] = acc_in[...]
    rel_out[...] = sum(back[p, B:].astype(F32) for p in range(32))
    for p in range(32):
        @pl.when(code[p] > 0)
        def _():
            acc[code[p] - 1] += back[p, :B].astype(F32)


def per_device(entities, relations, src_block, dst_member, dst_block, rel_id, neg_block, pos_mask):
    me = lax.axis_index("member")
    grp = lax.axis_index("group")
    blocks = entities.reshape(NB_DEV, B, D)
    mask = pos_mask[0, 0]

    match = dst_member[0] == me
    code = jnp.sum(jnp.where(match, dst_block[0] + 1, 0), axis=1)
    outgoing = call(pick_body, [SMEM, VMEM], tiles(32), 0)(code, blocks)
    received = lax.all_to_all(outgoing, "member", split_axis=0, concat_axis=0, tiled=True)

    src = lax.dynamic_index_in_dim(src_block[0], me, 0, keepdims=False)
    dst = lax.dynamic_index_in_dim(dst_member[0], me, 0, keepdims=False)
    rel = lax.dynamic_index_in_dim(rel_id[0], me, 0, keepdims=False)
    asked = lax.dynamic_index_in_dim(neg_block[:, 0, :], grp, 1, keepdims=False)
    order, org = routes(grp // 2, grp % 2)
    idx = jnp.concatenate([asked, org, src, dst, rel, order])

    sends = call(pre_body, [SMEM, VMEM], [tiles(7), tiles(6), tiles(2)], 0)(idx, blocks)
    mine, last = exchange(*sends)
    sums = sds(NB_DEV, B, D, dtype=F32)
    tile_store = pltpu.VMEM((TILES, B, D), BF16)
    stage = call(stage_body, [SMEM] + [VMEM] * 5, tiles(TILES * 2), 256, [tile_store])(
        idx, blocks, relations, mask, mine, last
    )
    back, gh = call(
        tile_body,
        [SMEM] + [VMEM] * 4,
        [sds(32, B + RELS * 8, D), tiles(TILES)],
        1600,
        [pltpu.VMEM((RELS, D, D), F32)] + [tile_store] * 2,
    )(idx, blocks, relations, received, stage)
    back, stage = lax.optimization_barrier((back, stage))
    back_in = lax.all_to_all(back, "member", split_axis=0, concat_axis=0, tiled=True)

    give, own, far, stays = call(
        neg_body,
        [SMEM] + [VMEM] * 3,
        [tiles(7), tiles(6), tiles(2), tiles(1)],
        512,
        [tile_store],
    )(idx, blocks, relations, stage)
    mine, last = exchange(give, own, far)
    acc = call(add_neg_body, [SMEM] + [VMEM] * 5, sums, 256)(
        idx, relations, gh, stays, mine, last
    )
    back_in, acc = lax.optimization_barrier((back_in, acc))
    out, relation_grad = call(
        add_dst_body,
        [SMEM] + [VMEM] * 2,
        [sums, sds(RELS * 8, D, dtype=F32)],
        1,
    )(code, acc, back_in)
    return out.reshape(NB_DEV * B, D), relation_grad.reshape(RELS, 8, D)


def solution(mesh):
    placed = (
        P(("group", "member"), None),
        P("group", None, None),
        P("group", None, None),
        P("group", None, None),
        P("group", None, None),
        P("group", None, None),
        P(None, "member", None),
        P("group", "member", None, None, None),
    )
    return jax.shard_map(
        per_device,
        mesh=mesh,
        in_specs=placed,
        out_specs=(P(("group", "member"), None), P("group", "member", None)),
        check_vma=False,
    )
```
